256 devices in a mesh: expert: 32 (over z, x_lo, core), tensor: 8 (over y, x_hi).
Axes of the slice: x: 4 (x_hi: 2, x_lo: 2; x = x_hi * 2 + x_lo), y: 4, z: 8, core: 2. Of those that a mesh axis runs over, the one named last changes fastest.
Arguments:
- tokens: bfloat16 [4096, 2880], P('expert', 'tensor'), may hold values from -6 to 6
- routes: int32 [4096, 4], P('expert'), may hold values from 0 to 31, all different within a row; in each aligned block of 128 rows (0 to 127, 128 to 255, ...) at most 32 rows name the same one
- gates: float32 [4096, 4], P('expert'), may hold values from 0.05 to 1
- gate_weight: bfloat16 [32, 2880, 2880], P('expert', None, 'tensor'), may hold values from -0.109375 to 0.109375
- up_weight: bfloat16 [32, 2880, 2880], P('expert', None, 'tensor'), may hold values from -0.109375 to 0.109375
- down_weight: bfloat16 [32, 2880, 2880], P('expert', 'tensor'), may hold values from -0.109375 to 0.109375
Outputs:
- mixed: bfloat16 [4096, 2880], P('expert', 'tensor')
The draws below stay inside these ranges and needn't reach their ends.
Inputs may be any that keep to these rules, and one draw needn't show every extreme that they name: `routes`: each row names 4 different experts. Among the 128 rows of one index of expert (aligned blocks of rows), no expert is named by more than 32 rows, a bound that some block reaches.
All inputs are finite; a program needn't handle non-finite values.
Results may differ from the reference program's by a relative error of at most 0.018.
Values may be sent and summed in bfloat16 or wider, within the bound.
A program may use at most 128 MiB of HBM per device.

```python
import math
import jax
import jax.numpy as jnp
import numpy as np
from jax import lax

D = 2880
FF = 2880
TOP = 4
TOK_DEV = 128
EXPERTS = 32
CAP = 32
TOKENS = 4096
N_EXPERT = 32
N_TENSOR = 8


def steps_of(key, dims, shards, low, largest):
    loudness = 1.0
    for dim, shards_of in shards:
        draws = jax.random.uniform(jax.random.fold_in(jax.random.fold_in(key, 6), dim), (shards_of,), jnp.float32, low / len(shards), largest / len(shards))
        loudness = loudness * jnp.repeat(jnp.exp(draws), dims[dim] // shards_of).reshape((-1,) + (1,) * (len(dims) - 1 - dim))
    return loudness


def assign_block(rng, own, number, rows, count, top, most, slope):
    ranking = jax.random.permutation(rng, count)
    crowded, usual = load_shares(count, rows * top, most, slope, True), load_shares(count, rows * top, most, slope, False)
    places = jnp.arange(count)

    def named(lengths, offset_by):
        used = int((lengths > 0).sum())
        fixed = max(1, used // 4)
        moved = fixed + (places - fixed + offset_by * (used - fixed)) % max(1, count - fixed)
        return jnp.zeros((count,), jnp.int32).at[ranking[jnp.where(places < fixed, places, moved)]].set(jnp.asarray(lengths, jnp.int32))

    lengths = jnp.where(number % 4 == 0, named(crowded, number // 4), named(usual, number - number // 4 - 1))
    mixed = jax.random.permutation(jax.random.fold_in(own, 3), count)
    giver, sink = mixed[0:count // 2 * 2:2], mixed[1:count // 2 * 2:2]
    margin = jnp.minimum(lengths[giver] - 1, most - lengths[sink]) // 2
    margin = jnp.where((giver == ranking[0]) | (sink == ranking[0]) | (lengths[sink] == 0), 0, jnp.maximum(margin, 0))
    moved = jax.random.randint(jax.random.fold_in(own, 4), (count // 2,), 0, 1 << 20) % (margin + 1)
    lengths = lengths.at[giver].add(-moved).at[sink].add(moved)
    labels = jnp.searchsorted(jnp.cumsum(lengths), jnp.arange(rows * top), side="right").astype(jnp.int32)
    listing = labels.reshape(top, rows).T
    listing = listing[jax.random.permutation(jax.random.fold_in(own, 1), rows)]
    offset_by = jax.random.randint(jax.random.fold_in(own, 2), (rows, 1), 0, top)
    return jnp.take_along_axis(listing, (jnp.arange(top)[None, :] + offset_by) % top, axis=1)


def load_shares(number_of, total, reach, skew, full):
    weights = [(1 << 20) // math.isqrt(rank ** skew) + 1 for rank in range(1, number_of + 1)]
    largest = reach if full else min(reach, max(-(-total // number_of), total * weights[0] // sum(weights)))
    least = 1 if total - largest >= number_of - 1 else 0
    holding, rest = [largest] + [least] * (number_of - 1), total - largest - least * (number_of - 1)
    while rest > 0:
        movable = [i for i in range(1, number_of) if holding[i] < largest] or [i for i in range(1, number_of) if holding[i] < reach]
        whole, budget = sum([weights[i] for i in movable]), rest
        for i in movable:
            more = min(reach - holding[i], max(1, budget * weights[i] // whole), rest)
            holding[i] = holding[i] + more
            rest = rest - more
    return np.array(holding)


def normal_values(own_key, dims, scale, reach, pieces=(), held_as=jnp.bfloat16):
    loudness = steps_of(own_key, dims, pieces, -0.22, 0.18) if pieces else 1.0
    array = jax.random.normal(own_key, dims, jnp.float32) * scale * loudness
    return jnp.minimum(jnp.maximum(array, -reach), reach).astype(held_as)


def setup_inputs(seed: int = 0) -> dict:
    seeds = jax.random.split(jax.random.key(seed), 7)
    tokens = normal_values(seeds[0], (TOKENS, D), 1.0, 6.0, ((0, 32), (1, 8)))
    routes_keys = jax.random.split(jax.random.fold_in(seeds[1], 1), TOKENS // TOK_DEV)
    routes_turns = jax.random.permutation(jax.random.fold_in(seeds[1], 3), TOKENS // TOK_DEV)
    routes = jax.vmap(lambda own, number: assign_block(jax.random.fold_in(seeds[1], 2), own, number, TOK_DEV, EXPERTS, TOP, CAP, 2))(routes_keys, routes_turns).reshape((TOKENS, TOP))
    gates = jnp.clip(jnp.exp(math.log(1.0) - 2.9957323 * jax.random.uniform(seeds[2], (TOKENS, TOP), jnp.float32) ** steps_of(seeds[2], (TOKENS, TOP), ((0, 32),), -0.2, 0.2)), 0.05, 1.0)
    gate_weight = normal_values(seeds[3], (EXPERTS, D, FF), D ** -0.5, 0.109375, ((0, 32), (2, 8)))
    up_weight = normal_values(seeds[4], (EXPERTS, D, FF), D ** -0.5, 0.109375, ((0, 32), (2, 8)))
    down_weight = normal_values(seeds[5], (EXPERTS, FF, D), FF ** -0.5, 0.109375, ((0, 32), (1, 8)))
    return {"tokens": tokens, "routes": routes, "gates": gates, "gate_weight": gate_weight, "up_weight": up_weight, "down_weight": down_weight}


def reference(tokens, routes, gates, gate_weight, up_weight, down_weight):
    per_block = TOK_DEV * TOP
    blocks = routes.reshape(N_EXPERT, per_block).astype(jnp.int32)
    onehot = (blocks[:, :, None] == jnp.arange(EXPERTS, dtype=jnp.int32)[None, None, :]).astype(jnp.int32)
    rank = jnp.cumsum(onehot, axis=1) - onehot
    slot = jnp.sum(rank * onehot, axis=2).astype(jnp.int32)
    source = jnp.broadcast_to(jnp.arange(N_EXPERT, dtype=jnp.int32)[:, None], (N_EXPERT, per_block))
    position = (source * CAP + slot).astype(jnp.int32)
    token_index = (jnp.arange(TOKENS * TOP, dtype=jnp.int32) // TOP).reshape(N_EXPERT, per_block)
    table = jnp.zeros((EXPERTS, N_EXPERT * CAP), jnp.int32).at[blocks, position].set(token_index)
    width = FF // N_TENSOR

    def expert_out(expert):
        rows = tokens[table[expert]]
        gate = jnp.dot(rows, gate_weight[expert], preferred_element_type=jnp.float32)
        up = jnp.dot(rows, up_weight[expert], preferred_element_type=jnp.float32)
        hidden = (jax.nn.silu(gate) * up).astype(jnp.bfloat16)
        hidden_blocks = hidden.reshape(N_EXPERT * CAP, N_TENSOR, width).astype(jnp.float32)
        down_blocks = down_weight[expert].reshape(N_TENSOR, width, D).astype(jnp.float32)
        parts = jnp.einsum('rnf,nfd->nrd', hidden_blocks, down_blocks)
        parts = lax.optimization_barrier(parts.astype(jnp.bfloat16)).astype(jnp.float32)
        return jnp.sum(parts, axis=0).astype(jnp.bfloat16)

    outputs = lax.map(expert_out, jnp.arange(EXPERTS, dtype=jnp.int32))
    picked = outputs[blocks, position].reshape(TOKENS, TOP, D).astype(jnp.float32)
    mixed = jnp.sum(picked * gates[:, :, None], axis=1)
    return mixed.astype(jnp.bfloat16)
```

```python
import jax
import jax.numpy as jnp
from jax import lax
from jax.experimental import pallas as pl
from jax.experimental.pallas import tpu as pltpu
from jax.sharding import PartitionSpec as P

BF = jnp.bfloat16
F32 = jnp.float32
MESH = pl.DeviceIdType.MESH
NZ = 8
CHUNK = 512
ORDER = (0, 1, 2, 4, 3, 5, 6, 7)
LAST = 6


def kernel(
    tok_ref, meta_ref, gw_ref, uw_ref, dw_ref, out_ref,
    tokpad, meta, zbuf, sbuf, xbuf, pf, pn, po, rf, rn, qbuf, rbuf, obuf, zr, zl,
    fin, fin32, fa, fb, gw, uw, dw, acc_g, acc_u, hid, ss, rs, ws,
):
    rows = tok_ref.shape[0]
    width = tok_ref.shape[1]
    half = rows // 2
    cap = rows // 4
    e = lax.axis_index("expert")
    t = lax.axis_index("tensor")
    z, xl, c = e // 4, (e // 2) % 2, e % 2
    y, xh = t // 2, t % 2

    def dev(z=z, xl=xl, c=c, t=t):
        return (z * 4 + xl * 2 + c, t)

    def tens(yy, hh):
        return yy * 2 + hh

    loads = [
        pltpu.make_async_copy(s, d, ws.at[i])
        for i, (s, d) in enumerate(((gw_ref, gw), (uw_ref, uw), (dw_ref, dw)))
    ]
    for load in loads:
        load.start()

    names = {}
    pending = []

    def sem(name, count=1):
        if name not in names:
            names[name] = names.get("", 0)
            names[""] = names[name] + count
        return names[name]

    def copy(name, src, dst, to, count=1, sent=0, got=0):
        i = sem(name, count)
        return pltpu.make_async_remote_copy(
            src_ref=src, dst_ref=dst, send_sem=ss.at[i + sent], recv_sem=rs.at[i + got],
            device_id=to, device_id_type=MESH,
        )

    def send(name, src, dst, to, **kw):
        cp = copy(name, src, dst, to, **kw)
        cp.start()
        pending.append(cp)

    def recv(name, dst, **kw):
        copy(name, dst, dst, dev(), **kw).wait_recv()

    def drain(keep):
        while len(pending) > keep:
            pending.pop(0).wait_send()

    y_up, y_dn = tens((y + 1) % 4, xh), tens((y + 3) % 4, xh)
    z_up, z_dn = (z + 1) % NZ, (z + NZ - 1) % NZ
    sides = [(cc, hh) for cc in range(2) for hh in range(2)]

    partners = [dev(t=(t + r) % 8) for r in range(1, 8)]
    partners += [dev(z=(z + r) % NZ) for r in range(1, NZ)]
    partners += [dev(c=1 - c)]
    partners += [dev(xl=1 - xl, c=cc, t=tens(y, hh)) for cc, hh in sides]
    barrier = pltpu.get_barrier_semaphore()
    for to in partners:
        pl.semaphore_signal(barrier, inc=1, device_id=to, device_id_type=MESH)

    tokpad[:, 256:384] = jnp.zeros((rows, 128), BF)
    tokpad[:, 0:width] = tok_ref[...]
    zbuf[z, 0, :, pl.ds(pl.multiple_of(256 * xh, 128), 256)] = tokpad[:, 0:256]
    btile = (z, 1 + t // 4, slice(None), pl.ds(pl.multiple_of(128 * (t % 4), 128), 128))
    zbuf[btile] = tokpad[:, 256:384]

    experts = 4 * NZ
    iota_e = lax.broadcasted_iota(jnp.int32, (experts, rows), 0).astype(F32)
    named = jnp.zeros((experts, rows), F32)
    for k in range(4):
        named = named + (iota_e == meta_ref[k : k + 1, :]).astype(F32)
    before = (
        lax.broadcasted_iota(jnp.int32, (rows, rows), 0)
        < lax.broadcasted_iota(jnp.int32, (rows, rows), 1)
    ).astype(F32)
    rank = jnp.dot(named.astype(BF), before.astype(BF), preferred_element_type=F32)
    for k in range(4):
        route = meta_ref[k : k + 1, :]
        slot = jnp.sum(jnp.where(iota_e == route, rank, 0.0), axis=0, keepdims=True)
        meta[z, k : k + 1, :] = cap * route + slot
    meta[z, 4:8, :] = meta_ref[4:8, :]

    pl.semaphore_wait(barrier, len(partners))

    a_ref = zbuf.at[z, 0, :, pl.ds(pl.multiple_of(256 * xh, 128), 256)]
    b_ref = zbuf.at[z, 1 + t // 4, :, pl.ds(pl.multiple_of(128 * (t % 4), 128), 128)]
    send("ta", a_ref, a_ref, dev(t=tens(y, 1 - xh)))
    for r in range(1, 8):
        send(f"tb{r}", b_ref, b_ref, dev(t=(t + r) % 8))
    for r in range(1, NZ):
        send(f"m{r}", meta.at[z], meta.at[z], dev(z=(z + r) % NZ))
    recv("ta", a_ref)
    for r in range(1, 8):
        recv(f"tb{r}", b_ref)

    def zpart(buf, index, k, up):
        if k < 4:
            return buf.at[index]
        return buf.at[index, :, pl.ds(0 if up else half, half), :]

    def ring_send(k):
        for up in (True, False):
            index = (z + NZ - (k - 1)) % NZ if up else (z + k - 1) % NZ
            ref = zpart(zbuf, index, k, up)
            send(f"z{k}{up}", ref, ref, dev(z=z_up if up else z_dn))

    def ring_wait(k):
        for up in (True, False):
            index = (z + NZ - k) % NZ if up else (z + k) % NZ
            recv(f"z{k}{up}", zpart(zbuf, index, k, up))

    iota_r = lax.broadcasted_iota(jnp.int32, (rows, rows), 0)
    own = pl.ds(pl.multiple_of(cap * (xl * 2 + c), cap), cap)
    pair = pl.ds(pl.multiple_of(cap * (xl * 2 + 1 - c), cap), cap)

    def side_rows(cc, side_x, hh):
        return pl.ds(pl.multiple_of(cap * (side_x * 2 + cc) + cap // 2 * hh, cap // 2), cap // 2)

    def pick(g):
        r = ORDER[g]
        src = (z + r) % NZ
        if r:
            recv(f"m{NZ - r}", meta.at[src])
        ids = (rows * z + iota_r).astype(F32)
        chosen = jnp.zeros((rows, rows), F32)
        for k in range(4):
            chosen = chosen + (meta[src, k : k + 1, :] == ids).astype(F32)
        chosen = chosen.astype(BF)
        for ch in range(3):
            sbuf[g, ch] = jnp.dot(chosen, zbuf[src, ch], preferred_element_type=F32).astype(BF)
        hand_out("x", g, sbuf, xbuf, dispatch=True)

    def hand_out(name, g, src, dst, dispatch):
        for i, (cc, hh) in enumerate(sides):
            send(
                f"{name}s{g}",
                src.at[g, :, side_rows(cc, 1 - xl, xh if dispatch else hh), :],
                dst.at[g, 0:3, side_rows(c, xl, xh), :],
                dev(xl=1 - xl, c=cc, t=tens(y, hh)),
                count=4, sent=i, got=2 * c + xh,
            )
        send(f"{name}p{g}", src.at[g, :, pair, :], dst.at[g, 0:3, own, :], dev(c=1 - c))
        for ch in range(3):
            dst[g, ch, own, :] = src[g, ch, own, :]

    def collect(name, g, dst):
        recv(f"{name}p{g}", dst.at[g, 0:3, pair, :])
        for i, (cc, hh) in enumerate(sides):
            recv(f"{name}s{g}", dst.at[g, 0:3, side_rows(cc, 1 - xl, hh), :], count=4, got=i)

    lo, hi = pl.ds(0, half), pl.ds(half, half)

    def spread(g):
        collect("x", g, xbuf)
        send(f"yu{g}", xbuf.at[g, 0], xbuf.at[g, 3], dev(t=y_up))
        send(f"yd{g}", xbuf.at[g, 0], xbuf.at[g, 4], dev(t=y_dn))

    def forward(g):
        recv(f"yu{g}", xbuf.at[g, 3])
        send(f"fu{g}", xbuf.at[g, 3, lo, :], xbuf.at[g, 5, lo, :], dev(t=y_up))
        recv(f"yd{g}", xbuf.at[g, 4])
        send(f"fd{g}", xbuf.at[g, 4, hi, :], xbuf.at[g, 5, hi, :], dev(t=y_dn))

    def expert(g):
        recv(f"fu{g}", xbuf.at[g, 5, lo, :])
        recv(f"fd{g}", xbuf.at[g, 5, hi, :])
        if g == 0:
            for load in loads:
                load.wait()
        acc_g[...] = jnp.zeros_like(acc_g)
        acc_u[...] = jnp.zeros_like(acc_u)

        def step(i, carry):
            w = i + 3
            w = jnp.where(i == 0, y, w)
            w = jnp.where(i == 3, (y + 3) % 4, w)
            w = jnp.where(i == 4, (y + 1) % 4, w)
            w = jnp.where(i == 5, (y + 2) % 4, w)
            x = xbuf[g, i]
            acc_g[...] += jnp.dot(x, gw[w], preferred_element_type=F32)
            acc_u[...] += jnp.dot(x, uw[w], preferred_element_type=F32)
            return carry

        lax.fori_loop(0, 6, step, 0)
        gate = acc_g[...]
        hid[...] = (gate / (1.0 + jnp.exp(-gate)) * acc_u[...]).astype(BF)

        def down(w):
            return jnp.dot(hid[...], dw[w], preferred_element_type=F32).astype(BF)

        pf[g] = down((y + 2) % 4)
        send(f"pu{g}", pf.at[g, lo, :], rf.at[g, lo, :], dev(t=y_up))
        send(f"pd{g}", pf.at[g, hi, :], rf.at[g, hi, :], dev(t=y_dn))
        pn[g, 0] = down((y + 1) % 4)
        pn[g, 1] = down((y + 3) % 4)
        po[g] = down(y)
        qbuf[g, 1] = down(4)
        qbuf[g, 2] = down(5)

    def relay(g):
        recv(f"pu{g}", rf.at[g, lo, :])
        pn[g, 0, lo, :] = (pn[g, 0, lo, :].astype(F32) + rf[g, lo, :].astype(F32)).astype(BF)
        send(f"nu{g}", pn.at[g, 0], rn.at[g, 0], dev(t=y_up))
        recv(f"pd{g}", rf.at[g, hi, :])
        pn[g, 1, hi, :] = (pn[g, 1, hi, :].astype(F32) + rf[g, hi, :].astype(F32)).astype(BF)
        send(f"nd{g}", pn.at[g, 1], rn.at[g, 1], dev(t=y_dn))

    def give_back(g):
        recv(f"nu{g}", rn.at[g, 0])
        recv(f"nd{g}", rn.at[g, 1])
        total = po[g].astype(F32) + rn[g, 0].astype(F32) + rn[g, 1].astype(F32)
        qbuf[g, 0] = total.astype(BF)
        hand_out("r", g, qbuf, rbuf, dispatch=False)

    def combine(g):
        collect("r", g, rbuf)
        r = ORDER[g]
        src = (z + r) % NZ
        group, place = iota_r // cap, iota_r % cap
        place = jnp.where(group // 2 == xl, place, cap // 2 * xh + place % (cap // 2))
        ids = (rows * z + cap * group + place).astype(F32)
        mix = jnp.zeros((rows, rows), F32)
        for k in range(4):
            hit = meta[src, k : k + 1, :] == ids
            mix = mix + jnp.where(hit, meta[src, 4 + k : 5 + k, :], 0.0)
        mix = mix.T.astype(BF)
        k = min(r, NZ - r)
        for ch in range(3):
            part = jnp.dot(mix, rbuf[g, ch], preferred_element_type=F32)
            if r == 0:
                fin32[ch] = part
            else:
                obuf[r, ch] = part.astype(BF)

    def chain(r):
        ups = (True, False) if r == 4 else (r < 4,)
        for up in ups:
            k = r if up else NZ - r
            buf = zr if up else zl
            if k < 4:
                which = pl.ds(0 if up else half, half) if k == 3 else pl.ds(0, rows)
                recv(f"c{k + 1}{up}", buf.at[k, :, which, :])
                for ch in range(3):
                    obuf[r, ch, which, :] = (
                        obuf[r, ch, which, :].astype(F32) + buf[k, ch, which, :].astype(F32)
                    ).astype(BF)
            which = pl.ds(0 if up else half, half) if k == 4 else pl.ds(0, rows)
            send(
                f"c{k}{up}", obuf.at[r, :, which, :], buf.at[k - 1, :, which, :],
                dev(z=z_up if up else z_dn),
            )

    stages = (pick, spread, forward, expert, relay, give_back, combine)
    chained = {3: (4,), 4: (3,), 5: (5, 2), 6: (6, 1), 7: (7,)}
    ring_send(1)
    arrive = {1: (1,), 2: (2,), 3: (3, 4)}
    for tick in range(len(ORDER) + len(stages) - 1):
        for k in arrive.get(tick, ()):
            ring_wait(k)
            if k < 4:
                ring_send(k + 1)
        for s in (0, 1, 2, 4, 5, 6, 3):
            g = tick - s
            if 0 <= g < len(ORDER):
                stages[s](g)
                if s == 6:
                    for r in chained.get(g, ()):
                        chain(r)
        drain(60)

    recv("c1True", zr.at[0])
    recv("c1False", zl.at[0])
    for ch in range(3):
        fin32[ch] = fin32[ch] + zr[0, ch].astype(F32) + zl[0, ch].astype(F32)
        fin[ch] = fin32[ch].astype(BF)
    send(
        "fa", fin.at[0, :, pl.ds(pl.multiple_of(256 * (1 - xh), 128), 256)], fa,
        dev(t=tens(y, 1 - xh)),
    )
    for r in range(1, 8):
        to = (t + r) % 8
        send(
            f"fb{r}",
            fin.at[1 + to // 4, :, pl.ds(pl.multiple_of(128 * (to % 4), 128), 128)],
            fb.at[r], dev(t=to),
        )
    drain(8)
    total = fin32[1 + t // 4, :, pl.ds(pl.multiple_of(128 * (t % 4), 128), 128)]
    for r in range(1, 8):
        recv(f"fb{r}", fb.at[r])
        total = total + fb[r].astype(F32)
    recv("fa", fa)
    first = fin32[0, :, pl.ds(pl.multiple_of(256 * xh, 128), 256)] + fa[...].astype(F32)
    out_ref[:, 0:256] = first.astype(BF)
    out_ref[:, 256:width] = total[:, 0 : width - 256].astype(BF)
    drain(0)


SEMS = 240


def body(tokens, routes, gates, gate_weight, up_weight, down_weight):
    rows, width = tokens.shape
    hidden = gate_weight.shape[2]
    meta = jnp.concatenate([routes.T.astype(F32), gates.T], axis=0)
    rest = 384 - width

    def by_rows(weight):
        parts = weight.reshape(8, width, hidden)
        first = parts[:, 0:256].reshape(4, CHUNK, hidden)
        last = jnp.pad(parts[:, 256:width], ((0, 0), (0, rest), (0, 0)))
        return jnp.concatenate([first, last.reshape(2, CHUNK, hidden)], axis=0)

    def by_columns(weight):
        parts = weight.reshape(hidden, 8, width)
        first = parts[:, :, 0:256].reshape(hidden, 4, CHUNK)
        last = jnp.pad(parts[:, :, 256:width], ((0, 0), (0, 0), (0, rest)))
        return jnp.concatenate([first, last.reshape(hidden, 2, CHUNK)], axis=1).transpose(1, 0, 2)

    gw, uw = by_rows(gate_weight[0]), by_rows(up_weight[0])
    dw = by_columns(down_weight[0])
    vmem = pl.BlockSpec(memory_space=pltpu.VMEM)
    hbm = pl.BlockSpec(memory_space=pl.ANY)

    def buf(*shape, dtype=BF):
        return pltpu.VMEM(shape, dtype)

    wide = (3, rows, CHUNK)
    return pl.pallas_call(
        kernel,
        out_shape=jax.ShapeDtypeStruct(tokens.shape, BF),
        in_specs=[vmem, vmem, hbm, hbm, hbm],
        out_specs=vmem,
        scratch_shapes=[
            buf(rows, 384),
            buf(NZ, 8, rows, dtype=F32),
            buf(NZ, *wide),
            buf(NZ, *wide),
            buf(NZ, 6, rows, CHUNK),
            buf(NZ, rows, CHUNK),
            buf(NZ, 2, rows, CHUNK),
            buf(NZ, rows, CHUNK),
            buf(NZ, rows, CHUNK),
            buf(NZ, 2, rows, CHUNK),
            buf(NZ, *wide),
            buf(NZ, *wide),
            buf(NZ, *wide),
            buf(4, *wide),
            buf(4, *wide),
            buf(*wide),
            buf(*wide, dtype=F32),
            buf(rows, 256),
            buf(8, rows, 128),
            buf(*gw.shape), buf(*uw.shape), buf(*dw.shape),
            buf(rows, hidden, dtype=F32), buf(rows, hidden, dtype=F32), buf(rows, hidden),
            pltpu.SemaphoreType.DMA((SEMS,)),
            pltpu.SemaphoreType.DMA((SEMS,)),
            pltpu.SemaphoreType.DMA((3,)),
        ],
        compiler_params=pltpu.CompilerParams(
            collective_id=0, has_side_effects=True, vmem_limit_bytes=60 << 20
        ),
    )(tokens, meta, gw, uw, dw)


def solution(mesh):
    return jax.shard_map(
        body,
        mesh=mesh,
        in_specs=(
            P("expert", "tensor"),
            P("expert", None),
            P("expert", None),
            P("expert", None, "tensor"),
            P("expert", None, "tensor"),
            P("expert", "tensor", None),
        ),
        out_specs=P("expert", "tensor"),
        check_vma=False,
    )
```

```python
import jax
import jax.numpy as jnp
from jax import lax
from jax.experimental import pallas as pl
from jax.experimental.pallas import tpu as pltpu
from jax.sharding import PartitionSpec as P

BF = jnp.bfloat16
F32 = jnp.float32
MESH = pl.DeviceIdType.MESH
NZ = 8
CHUNK = 512
ORDER = (0, 1, 2, 3, 4, 5, 6, 7)
SCHEDULE = (
    ("ring", "A", 0), ("ring", "B", 0), ("pick", "A", 0), ("ring", "A", 1), ("pick", "A", 7),
    ("spread", 0), ("spread", 7), ("pick", "A", 1), ("ring", "B", 1), ("settle",),
    ("ring", "A", 2), ("pick", "A", 2), ("forward", 7), ("forward", 0), ("pick", "A", 6),
    ("spread", 1), ("pick", "B", 1), ("spread", 6), ("spread", 2), ("ring", "A", 3),
    ("pick", "A", 3), ("pick", "A", 5), ("ring", "B", 2), ("pick", "B", 6), ("spread", 3),
    ("ring", "A", 4), ("pick", "A", 4), ("pick", "B", 0), ("spread", 5), ("spread", 4),
    ("forward", 6), ("ring", "B", 3), ("pick", "B", 5), ("pick", "B", 3), ("forward", 5),
    ("pick", "B", 7), ("forward", 2), ("pick", "B", 2), ("forward", 4), ("forward", 3),
    ("ring", "B", 4), ("pick", "B", 4), ("expert", 6), ("expert", 5), ("expert", 4), ("relay", 6),
    ("expert", 3), ("combine", "B", 5), ("combine", "B", 6), ("relay", 4), ("combine", "B", 4),
    ("chain", "B", 4), ("relay", 5), ("give", 6), ("relay", 3), ("expert", 2), ("forward", 1),
    ("combine", "B", 3), ("chain", "B", 5), ("give", 4), ("chain", "B", 3), ("expert", 0),
    ("combine", "B", 2), ("give", 5), ("give", 3), ("combine", "A", 4), ("chain", "A", 4),
    ("relay", 2), ("expert", 7), ("chain", "B", 6), ("expert", 1), ("combine", "A", 3),
    ("chain", "A", 3), ("combine", "A", 5), ("chain", "A", 5), ("relay", 7), ("combine", "A", 6),
    ("chain", "B", 2), ("give", 2), ("combine", "B", 1), ("relay", 1), ("combine", "A", 2),
    ("chain", "A", 2), ("relay", 0), ("combine", "B", 7), ("chain", "A", 6), ("give", 7),
    ("give", 1), ("chain", "B", 7), ("chain", "B", 1), ("combine", "A", 7), ("combine", "A", 1),
    ("give", 0), ("chain", "A", 1), ("chain", "A", 7), ("combine", "B", 0), ("combine", "A", 0),
)


def kernel(
    tok_ref, meta_ref, gw_ref, uw_ref, dw_ref, out_ref,
    tokpad, raw, meta, zbuf, sbuf, xbuf, pf, pn, po, rf, rn, qbuf, rbuf, obuf, zr, zl,
    fin, fin32, fa, fb, gw, uw, dw, hid, ss, rs, ws,
):
    width, rows = tok_ref.shape
    half = rows // 2
    cap = rows // 4
    e = lax.axis_index("expert")
    t = lax.axis_index("tensor")
    z, xl, c = e // 4, (e // 2) % 2, e % 2
    y, xh = t // 2, t % 2

    def dev(z=z, xl=xl, c=c, t=t):
        return (z * 4 + xl * 2 + c, t)

    def tens(yy, hh):
        return yy * 2 + hh

    loads = [
        pltpu.make_async_copy(s, d, ws.at[i])
        for i, (s, d) in enumerate(zip((gw_ref, uw_ref, dw_ref), (raw.at[0], raw.at[1], raw.at[2])))
    ]
    for load in loads:
        load.start()

    names = {}
    pending = []

    def sem(name, count=1):
        if name not in names:
            names[name] = names.get("", 0)
            names[""] = names[name] + count
        return names[name]

    def copy(name, src, dst, to, count=1, sent=0, got=0):
        i = sem(name, count)
        return pltpu.make_async_remote_copy(
            src_ref=src, dst_ref=dst, send_sem=ss.at[i + sent], recv_sem=rs.at[i + got],
            device_id=to, device_id_type=MESH,
        )

    def send(name, src, dst, to, **kw):
        cp = copy(name, src, dst, to, **kw)
        cp.start()
        pending.append(cp)

    def recv(name, dst, **kw):
        copy(name, dst, dst, dev(), **kw).wait_recv()

    def drain(keep):
        while len(pending) > keep:
            pending.pop(0).wait_send()

    y_up, y_dn = tens((y + 1) % 4, xh), tens((y + 3) % 4, xh)
    z_up, z_dn = (z + 1) % NZ, (z + NZ - 1) % NZ
    sides = [(cc, hh) for cc in range(2) for hh in range(2)]

    partners = [dev(t=(t + r) % 8) for r in range(1, 8)]
    partners += [dev(z=(z + r) % NZ) for r in range(1, NZ)]
    partners += [dev(c=1 - c)]
    partners += [dev(xl=1 - xl, c=cc, t=tens(y, hh)) for cc, hh in sides]
    barrier = pltpu.get_barrier_semaphore()
    for to in partners:
        pl.semaphore_signal(barrier, inc=1, device_id=to, device_id_type=MESH)

    tokpad[pl.ds(256, 128), :] = jnp.zeros((128, rows), F32)
    tokpad[pl.ds(0, width), :] = tok_ref[...].astype(F32)
    tok = tokpad[...].T.astype(BF)
    zbuf[z, 0, :, pl.ds(pl.multiple_of(256 * xh, 128), 256)] = tok[:, 0:256]
    btile = (z, 1 + t // 4, slice(None), pl.ds(pl.multiple_of(128 * (t % 4), 128), 128))
    zbuf[btile] = tok[:, 256:384]

    experts = 4 * NZ
    iota_e = lax.broadcasted_iota(jnp.int32, (experts, rows), 0).astype(F32)
    named = jnp.zeros((experts, rows), F32)
    for k in range(4):
        named = named + (iota_e == meta_ref[k : k + 1, :]).astype(F32)
    before = (
        lax.broadcasted_iota(jnp.int32, (rows, rows), 0)
        < lax.broadcasted_iota(jnp.int32, (rows, rows), 1)
    ).astype(F32)
    rank = jnp.dot(named.astype(BF), before.astype(BF), preferred_element_type=F32)
    for k in range(4):
        route = meta_ref[k : k + 1, :]
        slot = jnp.sum(jnp.where(iota_e == route, rank, 0.0), axis=0, keepdims=True)
        meta[z, k : k + 1, :] = cap * route + slot
    meta[z, 4:8, :] = meta_ref[4:8, :]

    pl.semaphore_wait(barrier, len(partners))

    a_ref = zbuf.at[z, 0, :, pl.ds(pl.multiple_of(256 * xh, 128), 256)]
    b_ref = zbuf.at[z, 1 + t // 4, :, pl.ds(pl.multiple_of(128 * (t % 4), 128), 128)]
    send("ta", a_ref, a_ref, dev(t=tens(y, 1 - xh)))
    for r in range(1, 8):
        send(f"tb{r}", b_ref, b_ref, dev(t=(t + r) % 8))
    for r in range(1, NZ):
        send(f"m{r}", meta.at[z], meta.at[z], dev(z=(z + r) % NZ))
    spans = {"A": (0,), "B": (1, 2)}

    def span(part):
        return pl.ds(0, 1) if part == "A" else pl.ds(1, 2)

    def zpart(buf, index, part, k, up):
        if k < 4:
            return buf.at[index, span(part)]
        return buf.at[index, span(part), pl.ds(0 if up else half, half), :]

    def ring(part, k):
        if k == 0:
            if part == "A":
                recv("ta", a_ref)
            else:
                for r in range(1, 8):
                    recv(f"tb{r}", b_ref)
        for up in (True, False):
            if k > 0:
                index = (z + NZ - k) % NZ if up else (z + k) % NZ
                recv(f"z{part}{k}{up}", zpart(zbuf, index, part, k, up))
            if k < 4:
                index = (z + NZ - k) % NZ if up else (z + k) % NZ
                ref = zpart(zbuf, index, part, k + 1, up)
                send(f"z{part}{k + 1}{up}", ref, ref, dev(z=z_up if up else z_dn))

    iota_r = lax.broadcasted_iota(jnp.int32, (rows, rows), 0)
    own = pl.ds(pl.multiple_of(cap * (xl * 2 + c), cap), cap)
    pair = pl.ds(pl.multiple_of(cap * (xl * 2 + 1 - c), cap), cap)

    def side_rows(cc, side_x, hh):
        return pl.ds(pl.multiple_of(cap * (side_x * 2 + cc) + cap // 2 * hh, cap // 2), cap // 2)

    def pick(part, g):
        r = ORDER[g]
        src = (z + r) % NZ
        if r and part == "A":
            recv(f"m{NZ - r}", meta.at[src])
        ids = (rows * z + iota_r).astype(F32)
        chosen = jnp.zeros((rows, rows), F32)
        for k in range(4):
            chosen = chosen + (meta[src, k : k + 1, :] == ids).astype(F32)
        chosen = chosen.astype(BF)
        for ch in spans[part]:
            sbuf[g, ch] = jnp.dot(chosen, zbuf[src, ch], preferred_element_type=F32).astype(BF)
        hand_out("x", part, g, sbuf, xbuf, dispatch=True)

    def hand_out(name, part, g, src, dst, dispatch):
        chs = span(part)
        for i, (cc, hh) in enumerate(sides):
            send(
                f"{name}s{part}{g}",
                src.at[g, chs, side_rows(cc, 1 - xl, xh if dispatch else hh), :],
                dst.at[g, chs, side_rows(c, xl, xh), :],
                dev(xl=1 - xl, c=cc, t=tens(y, hh)),
                count=4, sent=i, got=2 * c + xh,
            )
        send(f"{name}p{part}{g}", src.at[g, chs, pair, :], dst.at[g, chs, own, :], dev(c=1 - c))
        for ch in spans[part]:
            dst[g, ch, own, :] = src[g, ch, own, :]

    def collect(name, part, g, dst):
        chs = span(part)
        recv(f"{name}p{part}{g}", dst.at[g, chs, pair, :])
        for i, (cc, hh) in enumerate(sides):
            recv(f"{name}s{part}{g}", dst.at[g, chs, side_rows(cc, 1 - xl, hh), :], count=4, got=i)

    lo, hi = pl.ds(0, half), pl.ds(half, half)

    def settle():
        hidden = raw.shape[1]
        for i, to in enumerate((gw, uw, dw)):
            loads[i].wait()
            for s in range(8):
                first = raw[i, :, s * width : s * width + 256]
                last = raw[i, :, s * width + 256 : (s + 1) * width]
                at, low = pl.ds(256 * (s % 2), 256), 128 * (s % 4)
                if i < 2:
                    to[s // 2, at, :] = first.T
                    to[4 + s // 4, low : low + 128, :] = jnp.zeros((128, hidden), BF)
                    to[4 + s // 4, low : low + width - 256, :] = last.T
                else:
                    to[s // 2, :, at] = first
                    to[4 + s // 4, :, low : low + 128] = jnp.zeros((hidden, 128), BF)
                    to[4 + s // 4, :, low : low + width - 256] = last

    def spread(g):
        collect("x", "A", g, xbuf)
        send(f"yu{g}", xbuf.at[g, 0], xbuf.at[g, 3], dev(t=y_up))
        send(f"yd{g}", xbuf.at[g, 0], xbuf.at[g, 4], dev(t=y_dn))

    def forward(g):
        recv(f"yu{g}", xbuf.at[g, 3])
        send(f"fu{g}", xbuf.at[g, 3, lo, :], xbuf.at[g, 5, lo, :], dev(t=y_up))
        recv(f"yd{g}", xbuf.at[g, 4])
        send(f"fd{g}", xbuf.at[g, 4, hi, :], xbuf.at[g, 5, hi, :], dev(t=y_dn))

    def expert(g):
        recv(f"fu{g}", xbuf.at[g, 5, lo, :])
        recv(f"fd{g}", xbuf.at[g, 5, hi, :])
        collect("x", "B", g, xbuf)
        order = (y, 4, 5, (y + 3) % 4, (y + 1) % 4, (y + 2) % 4)

        def inner(weight):
            return sum(
                jnp.dot(xbuf[g, i], weight[w], preferred_element_type=F32)
                for i, w in enumerate(order)
            )

        gate = inner(gw)
        hid[...] = (gate / (1.0 + jnp.exp(-gate)) * inner(uw)).astype(BF)

        def down(w):
            return jnp.dot(hid[...], dw[w], preferred_element_type=F32).astype(BF)

        pf[g] = down((y + 2) % 4)
        send(f"pu{g}", pf.at[g, lo, :], rf.at[g, lo, :], dev(t=y_up))
        send(f"pd{g}", pf.at[g, hi, :], rf.at[g, hi, :], dev(t=y_dn))
        qbuf[g, 1] = down(4)
        qbuf[g, 2] = down(5)
        hand_out("r", "B", g, qbuf, rbuf, dispatch=False)
        pn[g, 0] = down((y + 1) % 4)
        pn[g, 1] = down((y + 3) % 4)
        po[g] = down(y)

    def relay(g):
        recv(f"pu{g}", rf.at[g, lo, :])
        pn[g, 0, lo, :] = (pn[g, 0, lo, :].astype(F32) + rf[g, lo, :].astype(F32)).astype(BF)
        send(f"nu{g}", pn.at[g, 0], rn.at[g, 0], dev(t=y_up))
        recv(f"pd{g}", rf.at[g, hi, :])
        pn[g, 1, hi, :] = (pn[g, 1, hi, :].astype(F32) + rf[g, hi, :].astype(F32)).astype(BF)
        send(f"nd{g}", pn.at[g, 1], rn.at[g, 1], dev(t=y_dn))

    def give_back(g):
        recv(f"nu{g}", rn.at[g, 0])
        recv(f"nd{g}", rn.at[g, 1])
        total = po[g].astype(F32) + rn[g, 0].astype(F32) + rn[g, 1].astype(F32)
        qbuf[g, 0] = total.astype(BF)
        hand_out("r", "A", g, qbuf, rbuf, dispatch=False)

    def combine(part, g):
        collect("r", part, g, rbuf)
        r = ORDER[g]
        src = (z + r) % NZ
        group, place = iota_r // cap, iota_r % cap
        place = jnp.where(group // 2 == xl, place, cap // 2 * xh + place % (cap // 2))
        ids = (rows * z + cap * group + place).astype(F32)
        mix = jnp.zeros((rows, rows), F32)
        for k in range(4):
            hit = meta[src, k : k + 1, :] == ids
            mix = mix + jnp.where(hit, meta[src, 4 + k : 5 + k, :], 0.0)
        mix = mix.T.astype(BF)
        for ch in spans[part]:
            mixed = jnp.dot(mix, rbuf[g, ch], preferred_element_type=F32)
            if r == 0:
                fin32[ch] = mixed
            else:
                obuf[r, ch] = mixed.astype(BF)

    def chain(part, r):
        chs = span(part)
        ups = (True, False) if r == 4 else (r < 4,)
        for up in ups:
            k = r if up else NZ - r
            buf = zr if up else zl
            if k < 4:
                which = pl.ds(0 if up else half, half) if k == 3 else pl.ds(0, rows)
                recv(f"c{part}{k + 1}{up}", buf.at[k, chs, which, :])
                for ch in spans[part]:
                    obuf[r, ch, which, :] = (
                        obuf[r, ch, which, :].astype(F32) + buf[k, ch, which, :].astype(F32)
                    ).astype(BF)
            which = pl.ds(0 if up else half, half) if k == 4 else pl.ds(0, rows)
            send(
                f"c{part}{k}{up}", obuf.at[r, chs, which, :], buf.at[k - 1, chs, which, :],
                dev(z=z_up if up else z_dn),
            )

    steps = {
        "ring": ring, "pick": pick, "spread": spread, "forward": forward, "expert": expert,
        "settle": settle, "relay": relay, "give": give_back, "combine": combine, "chain": chain,
    }
    for what, *args in SCHEDULE:
        steps[what](*args)
        drain(60)

    for part in "AB":
        recv(f"c{part}1True", zr.at[0, span(part)])
        recv(f"c{part}1False", zl.at[0, span(part)])
    for ch in range(3):
        fin32[ch] = fin32[ch] + zr[0, ch].astype(F32) + zl[0, ch].astype(F32)
        fin[ch] = fin32[ch].astype(BF)
    send(
        "fa", fin.at[0, :, pl.ds(pl.multiple_of(256 * (1 - xh), 128), 256)], fa,
        dev(t=tens(y, 1 - xh)),
    )
    for r in range(1, 8):
        to = (t + r) % 8
        send(
            f"fb{r}",
            fin.at[1 + to // 4, :, pl.ds(pl.multiple_of(128 * (to % 4), 128), 128)],
            fb.at[r], dev(t=to),
        )
    drain(8)
    total = fin32[1 + t // 4, :, pl.ds(pl.multiple_of(128 * (t % 4), 128), 128)]
    for r in range(1, 8):
        recv(f"fb{r}", fb.at[r])
        total = total + fb[r].astype(F32)
    recv("fa", fa)
    first = fin32[0, :, pl.ds(pl.multiple_of(256 * xh, 128), 256)] + fa[...].astype(F32)
    out_ref[pl.ds(0, 256), :] = first.T.astype(BF)
    out_ref[pl.ds(256, width - 256), :] = total.T[0 : width - 256, :].astype(BF)
    drain(0)


SEMS = 320


def body(tokens, routes, gates, gate_weight, up_weight, down_weight):
    rows, width = tokens.shape
    hidden = gate_weight.shape[2]
    meta = jnp.concatenate([routes.T.astype(F32), gates.T], axis=0)
    vmem = pl.BlockSpec(memory_space=pltpu.VMEM)
    hbm = pl.BlockSpec(memory_space=pl.ANY)

    def buf(*shape, dtype=BF):
        return pltpu.VMEM(shape, dtype)

    wide = (3, rows, CHUNK)
    out = pl.pallas_call(
        kernel,
        out_shape=jax.ShapeDtypeStruct((width, rows), BF),
        in_specs=[vmem, vmem, hbm, hbm, hbm],
        out_specs=vmem,
        scratch_shapes=[
            buf(384, rows, dtype=F32),
            buf(3, hidden, gate_weight.shape[1]),
            buf(NZ, 8, rows, dtype=F32),
            buf(NZ, *wide),
            buf(NZ, *wide),
            buf(NZ, 6, rows, CHUNK),
            buf(NZ, rows, CHUNK),
            buf(NZ, 2, rows, CHUNK),
            buf(NZ, rows, CHUNK),
            buf(NZ, rows, CHUNK),
            buf(NZ, 2, rows, CHUNK),
            buf(NZ, *wide),
            buf(NZ, *wide),
            buf(NZ, *wide),
            buf(4, *wide),
            buf(4, *wide),
            buf(*wide),
            buf(*wide, dtype=F32),
            buf(rows, 256),
            buf(8, rows, 128),
            buf(6, CHUNK, hidden), buf(6, CHUNK, hidden), buf(6, hidden, CHUNK),
            buf(rows, hidden),
            pltpu.SemaphoreType.DMA((SEMS,)),
            pltpu.SemaphoreType.DMA((SEMS,)),
            pltpu.SemaphoreType.DMA((3,)),
        ],
        compiler_params=pltpu.CompilerParams(
            collective_id=0, has_side_effects=True, vmem_limit_bytes=60 << 20
        ),
    )(tokens.T, meta, gate_weight[0].T, up_weight[0].T, down_weight[0])
    return out.T


def solution(mesh):
    return jax.shard_map(
        body,
        mesh=mesh,
        in_specs=(
            P("expert", "tensor"),
            P("expert", None),
            P("expert", None),
            P("expert", None, "tensor"),
            P("expert", None, "tensor"),
            P("expert", "tensor", None),
        ),
        out_specs=P("expert", "tensor"),
        check_vma=False,
    )
```

```python
import jax
import jax.numpy as jnp
from jax import lax
from jax.experimental import pallas as pl
from jax.experimental.pallas import tpu as pltpu
from jax.sharding import PartitionSpec as P

BF = jnp.bfloat16
F32 = jnp.float32
MESH = pl.DeviceIdType.MESH
NZ = 8
CHUNK = 512
ORDER = (0, 1, 2, 3, 4, 5, 6, 7)
SCHEDULE = (
    ("ring", "A", 0), ("pick", "A", 0), ("ring", "B", 0), ("ring", "A", 1), ("pick", "A", 1),
    ("ring", "C", 0), ("spread", 0), ("pick", "A", 7), ("spread", 1), ("forward", 0),
    ("ring", "A", 2), ("pick", "A", 2), ("ring", "B", 1), ("pick", "B", 0), ("pick", "A", 6),
    ("spread", 7), ("spread", 2), ("ring", "A", 3), ("pick", "A", 5), ("forward", 1),
    ("ring", "C", 1), ("pick", "A", 3), ("spread", 6), ("pick", "B", 1), ("ring", "B", 2),
    ("ring", "A", 4), ("spread", 5), ("spread", 3), ("pick", "A", 4), ("ring", "C", 2),
    ("pick", "B", 6), ("spread", 4), ("pick", "B", 2), ("ring", "B", 3), ("pick", "B", 7),
    ("forward", 5), ("forward", 2), ("forward", 6), ("ring", "C", 3), ("pick", "B", 5),
    ("expert", 1), ("pick", "B", 3), ("forward", 4), ("forward", 7), ("ring", "B", 4),
    ("forward", 3), ("ring", "C", 4), ("pick", "B", 4), ("expert", 5), ("expert", 6),
    ("expert", 4), ("combine", "B", 1), ("combine", "B", 5), ("relay", 5), ("expert", 3),
    ("combine", "B", 4), ("chain", "B", 4), ("chain", "C", 4), ("relay", 4), ("expert", 2),
    ("expert", 7), ("combine", "B", 3), ("chain", "B", 5), ("relay", 3), ("chain", "B", 3),
    ("chain", "C", 5), ("chain", "C", 3), ("give", 4), ("combine", "B", 6), ("relay", 6),
    ("relay", 2), ("give", 5), ("expert", 0), ("combine", "A", 4), ("chain", "A", 4),
    ("chain", "B", 6), ("give", 3), ("combine", "B", 2), ("combine", "A", 5), ("relay", 7),
    ("relay", 1), ("chain", "B", 2), ("give", 6), ("combine", "B", 7), ("chain", "A", 5),
    ("combine", "A", 3), ("chain", "A", 3), ("give", 2), ("chain", "C", 6), ("relay", 0),
    ("combine", "A", 6), ("chain", "B", 1), ("give", 7), ("chain", "A", 6), ("combine", "A", 2),
    ("chain", "A", 2), ("chain", "C", 2), ("combine", "B", 0), ("give", 1), ("combine", "A", 7),
    ("chain", "B", 7), ("give", 0), ("chain", "A", 7), ("combine", "A", 1), ("chain", "A", 1),
    ("combine", "A", 0), ("chain", "C", 1), ("chain", "C", 7), ("final", "A"), ("final", "B"),
)


def kernel(
    tok_ref, route_ref, gate_ref, gw_ref, uw_ref, dw_ref, out_ref,
    tokpad, raw, meta, zbuf, sbuf, xbuf, pf, pn, po, rf, rn, qbuf, rbuf, obuf, zr, zl,
    fin, fin32, fa, fb, gw, uw, dw, hid, ss, rs, ws,
):
    width, rows = tok_ref.shape
    half = rows // 2
    cap = rows // 4
    e = lax.axis_index("expert")
    t = lax.axis_index("tensor")
    z, xl, c = e // 4, (e // 2) % 2, e % 2
    y, xh = t // 2, t % 2

    def dev(z=z, xl=xl, c=c, t=t):
        return (z * 4 + xl * 2 + c, t)

    def tens(yy, hh):
        return yy * 2 + hh

    loads = [
        pltpu.make_async_copy(s, d, ws.at[i])
        for i, (s, d) in enumerate(zip((gw_ref, uw_ref, dw_ref), (raw.at[0], raw.at[1], raw.at[2])))
    ]
    for load in loads:
        load.start()

    names = {}
    pending = []

    def sem(name, count=1):
        if name not in names:
            names[name] = names.get("", 0)
            names[""] = names[name] + count
        return names[name]

    def copy(name, src, dst, to, count=1, sent=0, got=0):
        i = sem(name, count)
        return pltpu.make_async_remote_copy(
            src_ref=src, dst_ref=dst, send_sem=ss.at[i + sent], recv_sem=rs.at[i + got],
            device_id=to, device_id_type=MESH,
        )

    def send(name, src, dst, to, **kw):
        cp = copy(name, src, dst, to, **kw)
        cp.start()
        pending.append(cp)

    def recv(name, dst, **kw):
        copy(name, dst, dst, dev(), **kw).wait_recv()

    def drain(keep):
        while len(pending) > keep:
            pending.pop(0).wait_send()

    y_up, y_dn = tens((y + 1) % 4, xh), tens((y + 3) % 4, xh)
    z_up, z_dn = (z + 1) % NZ, (z + NZ - 1) % NZ
    sides = [(cc, hh) for cc in range(2) for hh in range(2)]

    partners = [dev(t=(t + r) % 8) for r in range(1, 8)]
    partners += [dev(z=(z + r) % NZ) for r in range(1, NZ)]
    partners += [dev(c=1 - c)]
    partners += [dev(xl=1 - xl, c=cc, t=tens(y, hh)) for cc, hh in sides]
    barrier = pltpu.get_barrier_semaphore()
    for to in partners:
        pl.semaphore_signal(barrier, inc=1, device_id=to, device_id_type=MESH)

    tokpad[pl.ds(256, 128), :] = jnp.zeros((128, rows), F32)
    tokpad[pl.ds(0, width), :] = tok_ref[...].astype(F32)
    tok = tokpad[...].T.astype(BF)
    zbuf[z, 0, :, pl.ds(pl.multiple_of(256 * xh, 128), 256)] = tok[:, 0:256]
    btile = (z, 1 + t // 4, slice(None), pl.ds(pl.multiple_of(128 * (t % 4), 128), 128))
    zbuf[btile] = tok[:, 256:384]

    experts = 4 * NZ
    iota_e = lax.broadcasted_iota(jnp.int32, (experts, rows), 0).astype(F32)
    chosen_by = [route_ref[k : k + 1, :].astype(F32) for k in range(4)]
    named = jnp.zeros((experts, rows), F32)
    for k in range(4):
        named = named + (iota_e == chosen_by[k]).astype(F32)
    before = (
        lax.broadcasted_iota(jnp.int32, (rows, rows), 0)
        < lax.broadcasted_iota(jnp.int32, (rows, rows), 1)
    ).astype(F32)
    rank = jnp.dot(named.astype(BF), before.astype(BF), preferred_element_type=F32)
    for k in range(4):
        route = chosen_by[k]
        slot = jnp.sum(jnp.where(iota_e == route, rank, 0.0), axis=0, keepdims=True)
        meta[z, k : k + 1, :] = cap * route + slot
    meta[z, 4:8, :] = gate_ref[...]

    pl.semaphore_wait(barrier, len(partners))

    a_ref = zbuf.at[z, 0, :, pl.ds(pl.multiple_of(256 * xh, 128), 256)]
    b_ref = zbuf.at[z, 1 + t // 4, :, pl.ds(pl.multiple_of(128 * (t % 4), 128), 128)]
    send("ta", a_ref, a_ref, dev(t=tens(y, 1 - xh)))
    for r in range(1, 8):
        send(f"tb{r}", b_ref, b_ref, dev(t=(t + r) % 8))
    for r in range(1, NZ):
        send(f"m{r}", meta.at[z], meta.at[z], dev(z=(z + r) % NZ))
    def settle():
        hidden = raw.shape[1]
        for i, to in enumerate((gw, uw, dw)):
            loads[i].wait()
            for s in range(8):
                first = raw[i, :, s * width : s * width + 256]
                last = raw[i, :, s * width + 256 : (s + 1) * width]
                at, low = pl.ds(256 * (s % 2), 256), 128 * (s % 4)
                if i < 2:
                    to[s // 2, at, :] = first.T
                    to[4 + s // 4, low : low + 128, :] = jnp.zeros((128, hidden), BF)
                    to[4 + s // 4, low : low + width - 256, :] = last.T
                else:
                    to[s // 2, :, at] = first
                    to[4 + s // 4, :, low : low + 128] = jnp.zeros((hidden, 128), BF)
                    to[4 + s // 4, :, low : low + width - 256] = last

    settle()

    spans = {"A": (0,), "B": (1, 2)}

    def span(part):
        return pl.ds(0, 1) if part == "A" else pl.ds(1, 2)

    chunk = {"A": 0, "B": 1, "C": 2}

    def zpart(buf, index, part, k, up):
        if k < 4:
            return buf.at[index, chunk[part]]
        return buf.at[index, chunk[part], pl.ds(0 if up else half, half), :]

    def ring(part, k):
        if k == 0:
            if part == "A":
                recv("ta", a_ref)
            elif part == "B":
                for r in range(1, 8):
                    recv(f"tb{r}", b_ref)
        for up in (True, False):
            if k > 0:
                index = (z + NZ - k) % NZ if up else (z + k) % NZ
                recv(f"z{part}{k}{up}", zpart(zbuf, index, part, k, up))
            if k < 4:
                index = (z + NZ - k) % NZ if up else (z + k) % NZ
                ref = zpart(zbuf, index, part, k + 1, up)
                send(f"z{part}{k + 1}{up}", ref, ref, dev(z=z_up if up else z_dn))

    iota_r = lax.broadcasted_iota(jnp.int32, (rows, rows), 0)
    own = pl.ds(pl.multiple_of(cap * (xl * 2 + c), cap), cap)
    pair = pl.ds(pl.multiple_of(cap * (xl * 2 + 1 - c), cap), cap)

    def side_rows(cc, side_x, hh):
        return pl.ds(pl.multiple_of(cap * (side_x * 2 + cc) + cap // 2 * hh, cap // 2), cap // 2)

    def pick(part, g):
        r = ORDER[g]
        src = (z + r) % NZ
        if r and part == "A":
            recv(f"m{NZ - r}", meta.at[src])
        ids = (rows * z + iota_r).astype(F32)
        chosen = jnp.zeros((rows, rows), F32)
        for k in range(4):
            chosen = chosen + (meta[src, k : k + 1, :] == ids).astype(F32)
        chosen = chosen.astype(BF)
        for ch in spans[part]:
            sbuf[g, ch] = jnp.dot(chosen, zbuf[src, ch], preferred_element_type=F32).astype(BF)
        hand_out("x", part, g, sbuf, xbuf, dispatch=True)

    def hand_out(name, part, g, src, dst, dispatch):
        chs = span(part)
        for i, (cc, hh) in enumerate(sides):
            send(
                f"{name}s{part}{g}",
                src.at[g, chs, side_rows(cc, 1 - xl, xh if dispatch else hh), :],
                dst.at[g, chs, side_rows(c, xl, xh), :],
                dev(xl=1 - xl, c=cc, t=tens(y, hh)),
                count=4, sent=i, got=2 * c + xh,
            )
        send(f"{name}p{part}{g}", src.at[g, chs, pair, :], dst.at[g, chs, own, :], dev(c=1 - c))
        for ch in spans[part]:
            dst[g, ch, own, :] = src[g, ch, own, :]

    def collect(name, part, g, dst):
        chs = span(part)
        recv(f"{name}p{part}{g}", dst.at[g, chs, pair, :])
        for i, (cc, hh) in enumerate(sides):
            recv(f"{name}s{part}{g}", dst.at[g, chs, side_rows(cc, 1 - xl, hh), :], count=4, got=i)

    lo, hi = pl.ds(0, half), pl.ds(half, half)

    def spread(g):
        collect("x", "A", g, xbuf)
        send(f"yu{g}", xbuf.at[g, 0], xbuf.at[g, 3], dev(t=y_up))
        send(f"yd{g}", xbuf.at[g, 0], xbuf.at[g, 4], dev(t=y_dn))

    def forward(g):
        recv(f"yu{g}", xbuf.at[g, 3])
        send(f"fu{g}", xbuf.at[g, 3, lo, :], xbuf.at[g, 5, lo, :], dev(t=y_up))
        recv(f"yd{g}", xbuf.at[g, 4])
        send(f"fd{g}", xbuf.at[g, 4, hi, :], xbuf.at[g, 5, hi, :], dev(t=y_dn))

    def expert(g):
        recv(f"fu{g}", xbuf.at[g, 5, lo, :])
        recv(f"fd{g}", xbuf.at[g, 5, hi, :])
        collect("x", "B", g, xbuf)
        order = (y, 4, 5, (y + 3) % 4, (y + 1) % 4, (y + 2) % 4)

        def inner(weight):
            return sum(
                jnp.dot(xbuf[g, i], weight[w], preferred_element_type=F32)
                for i, w in enumerate(order)
            )

        gate = inner(gw)
        hid[...] = (gate / (1.0 + jnp.exp(-gate)) * inner(uw)).astype(BF)

        def down(w):
            return jnp.dot(hid[...], dw[w], preferred_element_type=F32).astype(BF)

        pf[g] = down((y + 2) % 4)
        send(f"pu{g}", pf.at[g, lo, :], rf.at[g, lo, :], dev(t=y_up))
        send(f"pd{g}", pf.at[g, hi, :], rf.at[g, hi, :], dev(t=y_dn))
        qbuf[g, 1] = down(4)
        qbuf[g, 2] = down(5)
        hand_out("r", "B", g, qbuf, rbuf, dispatch=False)
        pn[g, 0] = down((y + 1) % 4)
        pn[g, 1] = down((y + 3) % 4)
        po[g] = down(y)

    def relay(g):
        recv(f"pu{g}", rf.at[g, lo, :])
        pn[g, 0, lo, :] = (pn[g, 0, lo, :].astype(F32) + rf[g, lo, :].astype(F32)).astype(BF)
        send(f"nu{g}", pn.at[g, 0], rn.at[g, 0], dev(t=y_up))
        recv(f"pd{g}", rf.at[g, hi, :])
        pn[g, 1, hi, :] = (pn[g, 1, hi, :].astype(F32) + rf[g, hi, :].astype(F32)).astype(BF)
        send(f"nd{g}", pn.at[g, 1], rn.at[g, 1], dev(t=y_dn))

    def give_back(g):
        recv(f"nu{g}", rn.at[g, 0])
        recv(f"nd{g}", rn.at[g, 1])
        total = po[g].astype(F32) + rn[g, 0].astype(F32) + rn[g, 1].astype(F32)
        qbuf[g, 0] = total.astype(BF)
        hand_out("r", "A", g, qbuf, rbuf, dispatch=False)

    def combine(part, g):
        collect("r", part, g, rbuf)
        r = ORDER[g]
        src = (z + r) % NZ
        group, place = iota_r // cap, iota_r % cap
        place = jnp.where(group // 2 == xl, place, cap // 2 * xh + place % (cap // 2))
        ids = (rows * z + cap * group + place).astype(F32)
        mix = jnp.zeros((rows, rows), F32)
        for k in range(4):
            hit = meta[src, k : k + 1, :] == ids
            mix = mix + jnp.where(hit, meta[src, 4 + k : 5 + k, :], 0.0)
        mix = mix.T.astype(BF)
        for ch in spans[part]:
            mixed = jnp.dot(mix, rbuf[g, ch], preferred_element_type=F32)
            if r == 0:
                fin32[ch] = mixed
            else:
                obuf[r, ch] = mixed.astype(BF)

    def chain(part, r):
        ch = chunk[part]
        ups = (True, False) if r == 4 else (r < 4,)
        for up in ups:
            k = r if up else NZ - r
            buf = zr if up else zl
            if k < 4:
                which = pl.ds(0 if up else half, half) if k == 3 else pl.ds(0, rows)
                recv(f"c{part}{k + 1}{up}", buf.at[k, ch, which, :])
                obuf[r, ch, which, :] = (
                    obuf[r, ch, which, :].astype(F32) + buf[k, ch, which, :].astype(F32)
                ).astype(BF)
            which = pl.ds(0 if up else half, half) if k == 4 else pl.ds(0, rows)
            send(
                f"c{part}{k}{up}", obuf.at[r, ch, which, :], buf.at[k - 1, ch, which, :],
                dev(z=z_up if up else z_dn),
            )

    def final(part):
        for one in "A" if part == "A" else "BC":
            recv(f"c{one}1True", zr.at[0, chunk[one]])
            recv(f"c{one}1False", zl.at[0, chunk[one]])
        for ch in spans[part]:
            fin32[ch] = fin32[ch] + zr[0, ch].astype(F32) + zl[0, ch].astype(F32)
            fin[ch] = fin32[ch].astype(BF)
        if part == "A":
            other = pl.ds(pl.multiple_of(256 * (1 - xh), 128), 256)
            send("fa", fin.at[0, :, other], fa, dev(t=tens(y, 1 - xh)))
            return
        for r in range(1, 8):
            to = (t + r) % 8
            send(
                f"fb{r}",
                fin.at[1 + to // 4, :, pl.ds(pl.multiple_of(128 * (to % 4), 128), 128)],
                fb.at[r], dev(t=to),
            )

    steps = {
        "ring": ring, "pick": pick, "spread": spread, "forward": forward, "expert": expert,
        "final": final, "relay": relay, "give": give_back, "combine": combine, "chain": chain,
    }
    for what, *args in SCHEDULE:
        steps[what](*args)
        drain(60)

    drain(8)
    total = fin32[1 + t // 4, :, pl.ds(pl.multiple_of(128 * (t % 4), 128), 128)]
    for r in range(1, 8):
        recv(f"fb{r}", fb.at[r])
        total = total + fb[r].astype(F32)
    recv("fa", fa)
    first = fin32[0, :, pl.ds(pl.multiple_of(256 * xh, 128), 256)] + fa[...].astype(F32)
    out_ref[pl.ds(0, 256), :] = first.T.astype(BF)
    out_ref[pl.ds(256, width - 256), :] = total.T[0 : width - 256, :].astype(BF)
    drain(0)


SEMS = 340


def body(tokens, routes, gates, gate_weight, up_weight, down_weight):
    rows, width = tokens.shape
    hidden = gate_weight.shape[2]
    vmem = pl.BlockSpec(memory_space=pltpu.VMEM)
    hbm = pl.BlockSpec(memory_space=pl.ANY)

    def buf(*shape, dtype=BF):
        return pltpu.VMEM(shape, dtype)

    wide = (3, rows, CHUNK)
    out = pl.pallas_call(
        kernel,
        out_shape=jax.ShapeDtypeStruct((width, rows), BF),
        in_specs=[vmem, vmem, vmem, hbm, hbm, hbm],
        out_specs=vmem,
        scratch_shapes=[
            buf(384, rows, dtype=F32),
            buf(3, hidden, gate_weight.shape[1]),
            buf(NZ, 8, rows, dtype=F32),
            buf(NZ, *wide),
            buf(NZ, *wide),
            buf(NZ, 6, rows, CHUNK),
            buf(NZ, rows, CHUNK),
            buf(NZ, 2, rows, CHUNK),
            buf(NZ, rows, CHUNK),
            buf(NZ, rows, CHUNK),
            buf(NZ, 2, rows, CHUNK),
            buf(NZ, *wide),
            buf(NZ, *wide),
            buf(NZ, *wide),
            buf(4, *wide),
            buf(4, *wide),
            buf(*wide),
            buf(*wide, dtype=F32),
            buf(rows, 256),
            buf(8, rows, 128),
            buf(6, CHUNK, hidden), buf(6, CHUNK, hidden), buf(6, hidden, CHUNK),
            buf(rows, hidden),
            pltpu.SemaphoreType.DMA((SEMS,)),
            pltpu.SemaphoreType.DMA((SEMS,)),
            pltpu.SemaphoreType.DMA((3,)),
        ],
        compiler_params=pltpu.CompilerParams(
            collective_id=0, has_side_effects=True, vmem_limit_bytes=60 << 20
        ),
    )(tokens.T, routes.T, gates.T, gate_weight[0].T, up_weight[0].T, down_weight[0])
    return out.T


def solution(mesh):
    return jax.shard_map(
        body,
        mesh=mesh,
        in_specs=(
            P("expert", "tensor"),
            P("expert", None),
            P("expert", None),
            P("expert", None, "tensor"),
            P("expert", None, "tensor"),
            P("expert", "tensor", None),
        ),
        out_specs=P("expert", "tensor"),
        check_vma=False,
    )
```

```python
import jax
import jax.numpy as jnp
from jax import lax
from jax.experimental import pallas as pl
from jax.experimental.pallas import tpu as pltpu
from jax.sharding import PartitionSpec as P

BF = jnp.bfloat16
F32 = jnp.float32
MESH = pl.DeviceIdType.MESH
NZ = 8
CHUNK = 512
ORDER = (0, 1, 2, 3, 4, 5, 6, 7)
SCHEDULE = (
    ("ring", "A", 0), ("pick", "A", 0), ("settle", 2), ("ring", "B", 0), ("ring", "A", 1), ("pick", "A", 1),
    ("ring", "C", 0), ("spread", 0), ("pick", "A", 7), ("spread", 1), ("forward", 0),
    ("ring", "A", 2), ("pick", "A", 2), ("ring", "B", 1), ("pick", "B", 0), ("pick", "A", 6),
    ("spread", 7), ("spread", 2), ("ring", "A", 3), ("pick", "A", 5), ("forward", 1),
    ("ring", "C", 1), ("pick", "A", 3), ("spread", 6), ("pick", "B", 1), ("ring", "B", 2),
    ("ring", "A", 4), ("spread", 5), ("spread", 3), ("pick", "A", 4), ("ring", "C", 2),
    ("pick", "B", 6), ("spread", 4), ("pick", "B", 2), ("ring", "B", 3), ("pick", "B", 7),
    ("forward", 5), ("forward", 2), ("forward", 6), ("ring", "C", 3), ("pick", "B", 5),
    ("expert", 1), ("pick", "B", 3), ("forward", 4), ("forward", 7), ("ring", "B", 4),
    ("forward", 3), ("ring", "C", 4), ("pick", "B", 4), ("expert", 5), ("expert", 6),
    ("expert", 4), ("combine", "B", 1), ("combine", "B", 5), ("relay", 5), ("expert", 3),
    ("combine", "B", 4), ("chain", "B", 4), ("chain", "C", 4), ("relay", 4), ("expert", 2),
    ("expert", 7), ("combine", "B", 3), ("chain", "B", 5), ("relay", 3), ("chain", "B", 3),
    ("chain", "C", 5), ("chain", "C", 3), ("give", 4), ("combine", "B", 6), ("relay", 6),
    ("relay", 2), ("give", 5), ("expert", 0), ("combine", "A", 4), ("chain", "A", 4),
    ("chain", "B", 6), ("give", 3), ("combine", "B", 2), ("combine", "A", 5), ("relay", 7),
    ("relay", 1), ("chain", "B", 2), ("give", 6), ("combine", "B", 7), ("chain", "A", 5),
    ("combine", "A", 3), ("chain", "A", 3), ("give", 2), ("chain", "C", 6), ("relay", 0),
    ("combine", "A", 6), ("chain", "B", 1), ("give", 7), ("chain", "A", 6), ("combine", "A", 2),
    ("chain", "A", 2), ("chain", "C", 2), ("combine", "B", 0), ("give", 1), ("combine", "A", 7),
    ("chain", "B", 7), ("give", 0), ("chain", "A", 7), ("combine", "A", 1), ("chain", "A", 1),
    ("combine", "A", 0), ("chain", "C", 1), ("chain", "C", 7), ("final", "A"), ("final", "B"),
)


def kernel(
    tok_ref, route_ref, gate_ref, gw_ref, uw_ref, dw_ref, out_ref,
    tokpad, raw, meta, zbuf, sbuf, xbuf, pf, pn, po, rf, rn, qbuf, rbuf, obuf, zr, zl,
    fin, fin32, fa, fb, gw, uw, dw, hid, ss, rs, ws,
):
    width, rows = tok_ref.shape
    half = rows // 2
    cap = rows // 4
    e = lax.axis_index("expert")
    t = lax.axis_index("tensor")
    z, xl, c = e // 4, (e // 2) % 2, e % 2
    y, xh = t // 2, t % 2

    def dev(z=z, xl=xl, c=c, t=t):
        return (z * 4 + xl * 2 + c, t)

    def tens(yy, hh):
        return yy * 2 + hh

    loads = [
        pltpu.make_async_copy(s, d, ws.at[i])
        for i, (s, d) in enumerate(zip((gw_ref, uw_ref, dw_ref), (raw.at[0], raw.at[1], raw.at[2])))
    ]
    for load in loads:
        load.start()

    names = {}
    pending = []

    def sem(name, count=1):
        if name not in names:
            names[name] = names.get("", 0)
            names[""] = names[name] + count
        return names[name]

    def copy(name, src, dst, to, count=1, sent=0, got=0):
        i = sem(name, count)
        return pltpu.make_async_remote_copy(
            src_ref=src, dst_ref=dst, send_sem=ss.at[i + sent], recv_sem=rs.at[i + got],
            device_id=to, device_id_type=MESH,
        )

    def send(name, src, dst, to, **kw):
        cp = copy(name, src, dst, to, **kw)
        cp.start()
        pending.append(cp)

    def recv(name, dst, **kw):
        copy(name, dst, dst, dev(), **kw).wait_recv()

    def drain(keep):
        while len(pending) > keep:
            pending.pop(0).wait_send()

    y_up, y_dn = tens((y + 1) % 4, xh), tens((y + 3) % 4, xh)
    z_up, z_dn = (z + 1) % NZ, (z + NZ - 1) % NZ
    sides = [(cc, hh) for cc in range(2) for hh in range(2)]

    partners = [dev(t=(t + r) % 8) for r in range(1, 8)]
    partners += [dev(z=(z + r) % NZ) for r in range(1, NZ)]
    partners += [dev(c=1 - c)]
    partners += [dev(xl=1 - xl, c=cc, t=tens(y, hh)) for cc, hh in sides]
    barrier = pltpu.get_barrier_semaphore()
    for to in partners:
        pl.semaphore_signal(barrier, inc=1, device_id=to, device_id_type=MESH)

    tokpad[pl.ds(256, 128), :] = jnp.zeros((128, rows), F32)
    tokpad[pl.ds(0, width), :] = tok_ref[...].astype(F32)
    tok = tokpad[...].T.astype(BF)
    zbuf[z, 0, :, pl.ds(pl.multiple_of(256 * xh, 128), 256)] = tok[:, 0:256]
    btile = (z, 1 + t // 4, slice(None), pl.ds(pl.multiple_of(128 * (t % 4), 128), 128))
    zbuf[btile] = tok[:, 256:384]

    experts = 4 * NZ
    iota_e = lax.broadcasted_iota(jnp.int32, (experts, rows), 0).astype(F32)
    chosen_by = [route_ref[k : k + 1, :].astype(F32) for k in range(4)]
    named = jnp.zeros((experts, rows), F32)
    for k in range(4):
        named = named + (iota_e == chosen_by[k]).astype(F32)
    before = (
        lax.broadcasted_iota(jnp.int32, (rows, rows), 0)
        < lax.broadcasted_iota(jnp.int32, (rows, rows), 1)
    ).astype(F32)
    rank = jnp.dot(named.astype(BF), before.astype(BF), preferred_element_type=F32)
    for k in range(4):
        route = chosen_by[k]
        slot = jnp.sum(jnp.where(iota_e == route, rank, 0.0), axis=0, keepdims=True)
        meta[z, k : k + 1, :] = cap * route + slot
    meta[z, 4:8, :] = gate_ref[...]

    pl.semaphore_wait(barrier, len(partners))

    a_ref = zbuf.at[z, 0, :, pl.ds(pl.multiple_of(256 * xh, 128), 256)]
    b_ref = zbuf.at[z, 1 + t // 4, :, pl.ds(pl.multiple_of(128 * (t % 4), 128), 128)]
    send("ta", a_ref, a_ref, dev(t=tens(y, 1 - xh)))
    for r in range(1, 8):
        send(f"tb{r}", b_ref, b_ref, dev(t=(t + r) % 8))
    for r in range(1, NZ):
        send(f"m{r}", meta.at[z], meta.at[z], dev(z=(z + r) % NZ))
    for up in (True, False):
        send(f"zh{up}", a_ref, a_ref, dev(z=z_up if up else z_dn))

    def settle(*which):
        hidden = raw.shape[1]
        for i in which:
            to = (gw, uw, dw)[i]
            loads[i].wait()
            for s in range(8):
                first = raw[i, :, s * width : s * width + 256]
                last = raw[i, :, s * width + 256 : (s + 1) * width]
                at, low = pl.ds(256 * (s % 2), 256), 128 * (s % 4)
                if i < 2:
                    to[s // 2, at, :] = first.T
                    to[4 + s // 4, low : low + 128, :] = jnp.zeros((128, hidden), BF)
                    to[4 + s // 4, low : low + width - 256, :] = last.T
                else:
                    to[s // 2, :, at] = first
                    to[4 + s // 4, :, low : low + 128] = jnp.zeros((hidden, 128), BF)
                    to[4 + s // 4, :, low : low + width - 256] = last

    settle(0, 1)

    mine = pl.ds(pl.multiple_of(256 * xh, 128), 256)
    theirs = pl.ds(pl.multiple_of(256 * (1 - xh), 128), 256)

    spans = {"A": (0,), "B": (1, 2)}

    def span(part):
        return pl.ds(0, 1) if part == "A" else pl.ds(1, 2)

    chunk = {"A": 0, "B": 1, "C": 2}

    def zpart(buf, index, part, k, up):
        if k < 4:
            return buf.at[index, chunk[part]]
        return buf.at[index, chunk[part], pl.ds(0 if up else half, half), :]

    def ring(part, k):
        if k == 0:
            if part == "A":
                recv("ta", a_ref)
            elif part == "B":
                for r in range(1, 8):
                    recv(f"tb{r}", b_ref)
        for up in (True, False):
            if k > 0:
                index = (z + NZ - k) % NZ if up else (z + k) % NZ
                if part == "A" and k == 1:
                    recv(f"zh{up}", zbuf.at[index, 0, :, mine])
                    recv(f"z{part}{k}{up}", zbuf.at[index, 0, :, theirs])
                else:
                    recv(f"z{part}{k}{up}", zpart(zbuf, index, part, k, up))
            if k < 4:
                index = (z + NZ - k) % NZ if up else (z + k) % NZ
                ref = zpart(zbuf, index, part, k + 1, up)
                if part == "A" and k == 0:
                    ref = zbuf.at[z, 0, :, theirs]
                send(f"z{part}{k + 1}{up}", ref, ref, dev(z=z_up if up else z_dn))

    iota_r = lax.broadcasted_iota(jnp.int32, (rows, rows), 0)
    own = pl.ds(pl.multiple_of(cap * (xl * 2 + c), cap), cap)
    pair = pl.ds(pl.multiple_of(cap * (xl * 2 + 1 - c), cap), cap)

    def side_rows(cc, side_x, hh):
        return pl.ds(pl.multiple_of(cap * (side_x * 2 + cc) + cap // 2 * hh, cap // 2), cap // 2)

    def pick(part, g):
        r = ORDER[g]
        src = (z + r) % NZ
        if r and part == "A":
            recv(f"m{NZ - r}", meta.at[src])
        ids = (rows * z + iota_r).astype(F32)
        chosen = jnp.zeros((rows, rows), F32)
        for k in range(4):
            chosen = chosen + (meta[src, k : k + 1, :] == ids).astype(F32)
        chosen = chosen.astype(BF)
        for ch in spans[part]:
            sbuf[g, ch] = jnp.dot(chosen, zbuf[src, ch], preferred_element_type=F32).astype(BF)
        hand_out("x", part, g, sbuf, xbuf, dispatch=True)

    def hand_out(name, part, g, src, dst, dispatch):
        chs = span(part)
        for i, (cc, hh) in enumerate(sides):
            send(
                f"{name}s{part}{g}",
                src.at[g, chs, side_rows(cc, 1 - xl, xh if dispatch else hh), :],
                dst.at[g, chs, side_rows(c, xl, xh), :],
                dev(xl=1 - xl, c=cc, t=tens(y, hh)),
                count=4, sent=i, got=2 * c + xh,
            )
        send(f"{name}p{part}{g}", src.at[g, chs, pair, :], dst.at[g, chs, own, :], dev(c=1 - c))
        for ch in spans[part]:
            dst[g, ch, own, :] = src[g, ch, own, :]

    def collect(name, part, g, dst):
        chs = span(part)
        recv(f"{name}p{part}{g}", dst.at[g, chs, pair, :])
        for i, (cc, hh) in enumerate(sides):
            recv(f"{name}s{part}{g}", dst.at[g, chs, side_rows(cc, 1 - xl, hh), :], count=4, got=i)

    lo, hi = pl.ds(0, half), pl.ds(half, half)

    def spread(g):
        collect("x", "A", g, xbuf)
        send(f"yu{g}", xbuf.at[g, 0], xbuf.at[g, 3], dev(t=y_up))
        send(f"yd{g}", xbuf.at[g, 0], xbuf.at[g, 4], dev(t=y_dn))

    def forward(g):
        recv(f"yu{g}", xbuf.at[g, 3])
        send(f"fu{g}", xbuf.at[g, 3, lo, :], xbuf.at[g, 5, lo, :], dev(t=y_up))
        recv(f"yd{g}", xbuf.at[g, 4])
        send(f"fd{g}", xbuf.at[g, 4, hi, :], xbuf.at[g, 5, hi, :], dev(t=y_dn))

    def expert(g):
        recv(f"fu{g}", xbuf.at[g, 5, lo, :])
        recv(f"fd{g}", xbuf.at[g, 5, hi, :])
        collect("x", "B", g, xbuf)
        order = (y, 4, 5, (y + 3) % 4, (y + 1) % 4, (y + 2) % 4)

        def inner(weight):
            return sum(
                jnp.dot(xbuf[g, i], weight[w], preferred_element_type=F32)
                for i, w in enumerate(order)
            )

        gate = inner(gw)
        hid[...] = (gate / (1.0 + jnp.exp(-gate)) * inner(uw)).astype(BF)

        def down(w):
            return jnp.dot(hid[...], dw[w], preferred_element_type=F32).astype(BF)

        pf[g] = down((y + 2) % 4)
        send(f"pu{g}", pf.at[g, lo, :], rf.at[g, lo, :], dev(t=y_up))
        send(f"pd{g}", pf.at[g, hi, :], rf.at[g, hi, :], dev(t=y_dn))
        qbuf[g, 1] = down(4)
        qbuf[g, 2] = down(5)
        hand_out("r", "B", g, qbuf, rbuf, dispatch=False)
        pn[g, 0] = down((y + 1) % 4)
        pn[g, 1] = down((y + 3) % 4)
        po[g] = down(y)

    def relay(g):
        recv(f"pu{g}", rf.at[g, lo, :])
        pn[g, 0, lo, :] = (pn[g, 0, lo, :].astype(F32) + rf[g, lo, :].astype(F32)).astype(BF)
        send(f"nu{g}", pn.at[g, 0], rn.at[g, 0], dev(t=y_up))
        recv(f"pd{g}", rf.at[g, hi, :])
        pn[g, 1, hi, :] = (pn[g, 1, hi, :].astype(F32) + rf[g, hi, :].astype(F32)).astype(BF)
        send(f"nd{g}", pn.at[g, 1], rn.at[g, 1], dev(t=y_dn))

    def give_back(g):
        recv(f"nu{g}", rn.at[g, 0])
        recv(f"nd{g}", rn.at[g, 1])
        total = po[g].astype(F32) + rn[g, 0].astype(F32) + rn[g, 1].astype(F32)
        qbuf[g, 0] = total.astype(BF)
        hand_out("r", "A", g, qbuf, rbuf, dispatch=False)

    def combine(part, g):
        collect("r", part, g, rbuf)
        r = ORDER[g]
        src = (z + r) % NZ
        group, place = iota_r // cap, iota_r % cap
        place = jnp.where(group // 2 == xl, place, cap // 2 * xh + place % (cap // 2))
        ids = (rows * z + cap * group + place).astype(F32)
        mix = jnp.zeros((rows, rows), F32)
        for k in range(4):
            hit = meta[src, k : k + 1, :] == ids
            mix = mix + jnp.where(hit, meta[src, 4 + k : 5 + k, :], 0.0)
        mix = mix.T.astype(BF)
        for ch in spans[part]:
            mixed = jnp.dot(mix, rbuf[g, ch], preferred_element_type=F32)
            if r == 0:
                fin32[ch] = mixed
            else:
                obuf[r, ch] = mixed.astype(BF)

    def chain(part, r):
        ch = chunk[part]
        ups = (True, False) if r == 4 else (r < 4,)
        for up in ups:
            k = r if up else NZ - r
            buf = zr if up else zl
            if k < 4:
                which = pl.ds(0 if up else half, half) if k == 3 else pl.ds(0, rows)
                recv(f"c{part}{k + 1}{up}", buf.at[k, ch, which, :])
                obuf[r, ch, which, :] = (
                    obuf[r, ch, which, :].astype(F32) + buf[k, ch, which, :].astype(F32)
                ).astype(BF)
            which = pl.ds(0 if up else half, half) if k == 4 else pl.ds(0, rows)
            send(
                f"c{part}{k}{up}", obuf.at[r, ch, which, :], buf.at[k - 1, ch, which, :],
                dev(z=z_up if up else z_dn),
            )

    def final(part):
        for one in "A" if part == "A" else "BC":
            recv(f"c{one}1True", zr.at[0, chunk[one]])
            recv(f"c{one}1False", zl.at[0, chunk[one]])
        for ch in spans[part]:
            fin32[ch] = fin32[ch] + zr[0, ch].astype(F32) + zl[0, ch].astype(F32)
            fin[ch] = fin32[ch].astype(BF)
        if part == "A":
            other = pl.ds(pl.multiple_of(256 * (1 - xh), 128), 256)
            send("fa", fin.at[0, :, other], fa, dev(t=tens(y, 1 - xh)))
            return
        for r in range(1, 8):
            to = (t + r) % 8
            send(
                f"fb{r}",
                fin.at[1 + to // 4, :, pl.ds(pl.multiple_of(128 * (to % 4), 128), 128)],
                fb.at[r], dev(t=to),
            )

    steps = {
        "ring": ring, "pick": pick, "spread": spread, "forward": forward, "expert": expert,
        "final": final, "settle": settle, "relay": relay, "give": give_back, "combine": combine, "chain": chain,
    }
    for what, *args in SCHEDULE:
        steps[what](*args)
        drain(120)

    drain(8)
    total = fin32[1 + t // 4, :, pl.ds(pl.multiple_of(128 * (t % 4), 128), 128)]
    for r in range(1, 8):
        recv(f"fb{r}", fb.at[r])
        total = total + fb[r].astype(F32)
    recv("fa", fa)
    first = fin32[0, :, pl.ds(pl.multiple_of(256 * xh, 128), 256)] + fa[...].astype(F32)
    out_ref[pl.ds(0, 256), :] = first.T.astype(BF)
    out_ref[pl.ds(256, width - 256), :] = total.T[0 : width - 256, :].astype(BF)
    drain(0)


SEMS = 340


def body(tokens, routes, gates, gate_weight, up_weight, down_weight):
    rows, width = tokens.shape
    hidden = gate_weight.shape[2]
    vmem = pl.BlockSpec(memory_space=pltpu.VMEM)
    hbm = pl.BlockSpec(memory_space=pl.ANY)

    def buf(*shape, dtype=BF):
        return pltpu.VMEM(shape, dtype)

    wide = (3, rows, CHUNK)
    out = pl.pallas_call(
        kernel,
        out_shape=jax.ShapeDtypeStruct((width, rows), BF),
        in_specs=[vmem, vmem, vmem, hbm, hbm, hbm],
        out_specs=vmem,
        scratch_shapes=[
            buf(384, rows, dtype=F32),
            buf(3, hidden, gate_weight.shape[1]),
            buf(NZ, 8, rows, dtype=F32),
            buf(NZ, *wide),
            buf(NZ, *wide),
            buf(NZ, 6, rows, CHUNK),
            buf(NZ, rows, CHUNK),
            buf(NZ, 2, rows, CHUNK),
            buf(NZ, rows, CHUNK),
            buf(NZ, rows, CHUNK),
            buf(NZ, 2, rows, CHUNK),
            buf(NZ, *wide),
            buf(NZ, *wide),
            buf(NZ, *wide),
            buf(4, *wide),
            buf(4, *wide),
            buf(*wide),
            buf(*wide, dtype=F32),
            buf(rows, 256),
            buf(8, rows, 128),
            buf(6, CHUNK, hidden), buf(6, CHUNK, hidden), buf(6, hidden, CHUNK),
            buf(rows, hidden),
            pltpu.SemaphoreType.DMA((SEMS,)),
            pltpu.SemaphoreType.DMA((SEMS,)),
            pltpu.SemaphoreType.DMA((3,)),
        ],
        compiler_params=pltpu.CompilerParams(
            collective_id=0, has_side_effects=True, vmem_limit_bytes=60 << 20
        ),
    )(tokens.T, routes.T, gates.T, gate_weight[0].T, up_weight[0].T, down_weight[0])
    return out.T


def solution(mesh):
    return jax.shard_map(
        body,
        mesh=mesh,
        in_specs=(
            P("expert", "tensor"),
            P("expert", None),
            P("expert", None),
            P("expert", None, "tensor"),
            P("expert", None, "tensor"),
            P("expert", "tensor", None),
        ),
        out_specs=P("expert", "tensor"),
        check_vma=False,
    )
```
